32 devices in a mesh: occ: 4 (over y, x), aux: 8 (over z, core).
Axes of the slice: x: 2, y: 2, z: 4, core: 2. Of those that a mesh axis runs over, the one named last changes fastest.
Arguments:
- factors: float32 [8192, 4, 768], P('aux', 'occ'), may hold values from -1.5 to 1.5
- eps_occ: float32 [4], replicated, may hold values from -2 to -0.5
- eps_vir: float32 [768], replicated, may hold values from 0.5 to 3
Outputs:
- density: float32 [8192, 4, 768], P('aux', 'occ')
The draws below stay inside these ranges and needn't reach their ends.
All inputs are finite; a program needn't handle non-finite values.
Results may differ from the reference program's by a relative error of at most 0.0003.
Values sent between devices are 32-bit elements; how exact they have to be, the bound alone decides.
A program may use at most 128 MiB of HBM per device.

```python
import jax
import jax.numpy as jnp
from jax import lax

OCC_DEV = 1
NV = 768
NAUX = 8192
NOCC = 4
N_OCC = 4


def block_scale(stream_key, extent, shards, smallest, largest):
    loudness = 1.0
    for axis_at, shards_of in shards:
        heights = jax.random.uniform(jax.random.fold_in(jax.random.fold_in(stream_key, 6), axis_at), (shards_of,), jnp.float32, smallest / len(shards), largest / len(shards))
        loudness = loudness * jnp.repeat(jnp.exp(heights), extent[axis_at] // shards_of).reshape((-1,) + (1,) * (len(extent) - 1 - axis_at))
    return loudness


def centred(stream_key, dims, spread, most, shards=(), kind=jnp.bfloat16):
    factor_of = block_scale(stream_key, dims, shards, -0.22, 0.18) if shards else 1.0
    result = jax.random.normal(stream_key, dims, jnp.float32) * spread * factor_of
    return jnp.minimum(jnp.maximum(result, -most), most).astype(kind)


def setup_inputs(seed: int = 0) -> dict:
    seeds = jax.random.split(jax.random.key(seed), 4)
    factors = centred(seeds[0], (NAUX, NOCC, NV), (1.0 / (NAUX ** 0.25)), 1.5, ((0, 8), (1, 4)), jnp.float32)
    eps_occ = jnp.clip(jax.random.uniform(seeds[1], (NOCC,), jnp.float32, -2.0, -0.5), -2.0, -0.5)
    eps_vir = jnp.clip(jax.random.uniform(seeds[2], (NV,), jnp.float32, 0.5, 3.0), 0.5, 3.0)
    return dict(factors=factors, eps_occ=eps_occ, eps_vir=eps_vir)


def reference(factors, eps_occ, eps_vir):
    width = OCC_DEV * NV
    flat = factors.reshape(NAUX, N_OCC, width)
    energies = eps_occ.reshape(N_OCC, OCC_DEV)

    def pair_vals(group):
        occ_part = lax.dynamic_index_in_dim(energies, group, 0, keepdims=False)
        return (occ_part[:, None] - eps_vir[None, :]).reshape(width)

    def one_group(group):
        own = lax.dynamic_index_in_dim(flat, group, 1, keepdims=False)
        own_vals = pair_vals(group)
        total = jnp.zeros((NAUX, width), jnp.float32)
        for offset in (-1, 0, 1):
            partner = ((group + offset + N_OCC) % N_OCC).astype(jnp.int32)
            other = lax.dynamic_index_in_dim(flat, partner, 1, keepdims=False)
            other_vals = pair_vals(partner)
            integral = jnp.dot(own.T, other, precision=lax.Precision.HIGHEST, preferred_element_type=jnp.float32)
            amplitude = integral / (own_vals[:, None] + other_vals[None, :])
            total = total + jnp.dot(other, amplitude.T, precision=lax.Precision.HIGHEST, preferred_element_type=jnp.float32)
        return 1.3 * total

    groups = lax.map(one_group, jnp.arange(N_OCC, dtype=jnp.int32))
    return jnp.transpose(groups, (1, 0, 2)).reshape(NAUX, N_OCC * OCC_DEV, NV)
```

```python
import functools

import jax
import jax.numpy as jnp
from jax import lax
from jax.experimental import pallas as pl
from jax.experimental.pallas import tpu as pltpu
from jax.sharding import PartitionSpec as P

MESH = pl.DeviceIdType.MESH
WIDE = 128
SPLIT = 2
PASS_ROWS = 384


def split_two(value):
    high = value.astype(jnp.bfloat16)
    return high, (value - high.astype(jnp.float32)).astype(jnp.bfloat16)


def mm(left, right):
    return jnp.dot(left, right, preferred_element_type=jnp.float32)


def kernel(
    own, occ, vir_row, vir_col, out,
    near, own_hi, own_lo, part, from_core, from_end, from_mid, red, amp, lhs, amp_hi, amp_lo,
    x_send, x_recv, y_send, y_recv, c_send, c_recv, e_send, e_recv, m_send, m_recv, b_send, b_recv, t_send, t_recv,
):
    rows, virt = own.shape
    nc = virt // WIDE
    half = WIDE // 2
    sub = rows // SPLIT
    g = lax.axis_index("occ")
    q = lax.axis_index("aux")
    z = q // 2
    core = q % 2
    g_x = g + 1 - 2 * (g % 2)
    g_y = (g + 2) % 4
    g_d = (g_x + 2) % 4
    q_core = q + 1 - 2 * core
    q_end = (z + 1 - 2 * (z % 2)) * 2 + core
    q_mid = (3 - z) * 2 + core
    is_mid = jnp.logical_or(z == 1, z == 2)
    is_end = jnp.logical_or(z == 0, z == 3)
    mine = pl.ds(pl.multiple_of(core * half, half), half)
    theirs = pl.ds(pl.multiple_of((1 - core) * half, half), half)

    barrier = pltpu.get_barrier_semaphore()
    for target in ({"occ": g_x}, {"occ": g_y}, {"aux": q_core}, {"aux": q_end}, {"aux": q_mid}):
        pl.semaphore_signal(barrier, inc=1, device_id=target, device_id_type=MESH)
    pl.semaphore_wait(barrier, 5)

    def remote(src, dst, send, recv, target):
        return pltpu.make_async_remote_copy(
            src_ref=src, dst_ref=dst, send_sem=send, recv_sem=recv, device_id=target, device_id_type=MESH
        )

    def x_copy(s):
        k, r = s // SPLIT, pl.ds((s % SPLIT) * sub, sub)
        return remote(own.at[r, pl.ds(k * WIDE, WIDE)], near.at[k, r], x_send.at[s], x_recv.at[s], {"occ": g_x})

    def y_copy(s):
        k, r = s // SPLIT, pl.ds((s % SPLIT) * sub, sub)
        return remote(near.at[k, r], near.at[nc + k, r], y_send.at[s], y_recv.at[s], {"occ": g_y})

    def core_copy(i):
        return remote(part.at[i, theirs], from_core.at[i], c_send.at[i], c_recv.at[i], {"aux": q_core})

    def end_copy(i):
        return remote(red.at[i], from_end.at[i], e_send.at[i], e_recv.at[i], {"aux": q_end})

    def mid_copy(i):
        return remote(red.at[i], from_mid.at[i], m_send.at[i], m_recv.at[i], {"aux": q_mid})

    def back_copy(i):
        return remote(amp.at[i, mine], amp.at[i, mine], b_send.at[i], b_recv.at[i], {"aux": q_end})

    def twin_copy(i):
        return remote(amp.at[i, mine], amp.at[i, mine], t_send.at[i], t_recv.at[i], {"aux": q_core})

    for s in range(nc * SPLIT):
        x_copy(s).start()

    tile = min(256, rows)

    def prepare(m, carry):
        r = pl.ds(pl.multiple_of(m * tile, tile), tile)
        high, low = split_two(own[r, :])
        own_hi[r, :] = high
        own_lo[r, :] = low
        out[r, :] = jnp.zeros((tile, virt), jnp.float32)
        return carry

    lax.fori_loop(0, rows // tile, prepare, 0)

    def chunk(i, r):
        if i < nc:
            return own[r, i * WIDE : (i + 1) * WIDE]
        return near[i - nc, r, :]

    def integral(i):
        high, low = split_two(chunk(i, slice(None)).T)
        lhs[:WIDE, :] = high
        lhs[WIDE:, :] = low
        for n in range(0, virt, 256):
            both = mm(lhs[...], own_hi[:, n : n + 256])
            part[i, :, n : n + 256] = both[:WIDE] + both[WIDE:] + mm(lhs[:WIDE, :], own_lo[:, n : n + 256])
        core_copy(i).start()

    def reduce_cores(i):
        core_copy(i).wait_recv()
        red[i] = part[i, mine, :] + from_core[i]

        @pl.when(is_end)
        def _():
            end_copy(i).start()

    def reduce_line(i):
        @pl.when(is_mid)
        def _():
            end_copy(i).wait_recv()
            red[i] = red[i] + from_end[i]
            mid_copy(i).start()

    def amplitude(i):
        @pl.when(is_mid)
        def _():
            mid_copy(i).wait_recv()
            other = occ[(g, g_x, g_d)[i // nc]]
            first = (i % nc) * WIDE + core * half
            col = vir_col[pl.ds(pl.multiple_of(first, half), half), :]
            denom = (occ[g] - vir_row[...]) + (other - col)
            amp[i, mine, :] = 1.3 * (red[i] + from_mid[i]) / denom
            back_copy(i).start()
            twin_copy(i).start()

    def arrived(i):
        @pl.when(is_end)
        def _():
            back_copy(i).wait_recv()
            twin_copy(i).start()

    def density(i):
        for j in (i - 1, i):
            twin_copy(j).wait_recv()
        high, low = split_two(amp[i - 1 : i + 1].reshape(2 * WIDE, virt))
        amp_hi[...] = high
        amp_lo[...] = low

        def add(m, carry):
            r = pl.ds(pl.multiple_of(m * tile, tile), tile)
            bh, bl = split_two(jnp.concatenate([chunk(i - 1, r), chunk(i, r)], axis=1))
            out[r, :] += mm(bh, amp_hi[...]) + mm(bl, amp_hi[...]) + mm(bh, amp_lo[...])
            return carry

        lax.fori_loop(0, rows // tile, add, 0)

    order = list(range(nc)) + [nc]
    for k in range(1, nc):
        order += [nc + k, 2 * nc + k - 1]
    order.append(3 * nc - 1)

    forwarded = 0
    for t in range(len(order) + 9):
        if 0 <= t - 8 < len(order) and order[t - 8] % 2 == 1:
            density(order[t - 8])
        if 0 <= t - 6 < len(order):
            arrived(order[t - 6])
        if 0 <= t - 4 < len(order):
            amplitude(order[t - 4])
        if 0 <= t - 2 < len(order):
            reduce_line(order[t - 2])
        if t < len(order):
            i = order[t]
            if i >= nc and forwarded < nc * SPLIT:
                last = (i - nc + 1) * SPLIT if i < 2 * nc else (i - 2 * nc + 1) * SPLIT + 1
                while forwarded < min(last, nc * SPLIT):
                    x_copy(forwarded).wait_recv()
                    y_copy(forwarded).start()
                    forwarded += 1
            if i >= 2 * nc:
                for s in range((i - 2 * nc) * SPLIT, (i - 2 * nc + 1) * SPLIT):
                    y_copy(s).wait_recv()
            integral(i)
            reduce_cores(i)

    for s in range(nc * SPLIT):
        x_copy(s).wait_send()
        y_copy(s).wait_send()
    for i in range(3 * nc):
        core_copy(i).wait_send()
        twin_copy(i).wait_send()

    @pl.when(is_end)
    def _():
        for i in range(3 * nc):
            end_copy(i).wait_send()

    @pl.when(is_mid)
    def _():
        for i in range(3 * nc):
            mid_copy(i).wait_send()
            back_copy(i).wait_send()


def line_body(factors, eps_occ, eps_vir):
    rows, _, virt = factors.shape
    nc = virt // WIDE
    items = 3 * nc
    f32, bf16 = jnp.float32, jnp.bfloat16
    dma = pltpu.SemaphoreType.DMA
    vmem = pl.BlockSpec(memory_space=pltpu.VMEM)
    result = pl.pallas_call(
        kernel,
        out_shape=jax.ShapeDtypeStruct((rows, virt), f32),
        in_specs=[vmem, pl.BlockSpec(memory_space=pltpu.SMEM), vmem, vmem],
        out_specs=vmem,
        scratch_shapes=[
            pltpu.VMEM((2 * nc, rows, WIDE), f32),
            pltpu.VMEM((rows, virt), bf16),
            pltpu.VMEM((rows, virt), bf16),
            pltpu.VMEM((items, WIDE, virt), f32),
            pltpu.VMEM((items, WIDE // 2, virt), f32),
            pltpu.VMEM((items, WIDE // 2, virt), f32),
            pltpu.VMEM((items, WIDE // 2, virt), f32),
            pltpu.VMEM((items, WIDE // 2, virt), f32),
            pltpu.VMEM((items, WIDE, virt), f32),
            pltpu.VMEM((2 * WIDE, rows), bf16),
            pltpu.VMEM((2 * WIDE, virt), bf16),
            pltpu.VMEM((2 * WIDE, virt), bf16),
        ]
        + [dma((nc * SPLIT,))] * 4
        + [dma((items,))] * 10,
        compiler_params=pltpu.CompilerParams(
            collective_id=0, has_side_effects=True, vmem_limit_bytes=58 * 1024 * 1024
        ),
        cost_estimate=pl.CostEstimate(
            flops=36 * rows * virt * virt, bytes_accessed=8 * rows * virt, transcendentals=0
        ),
    )(factors.reshape(rows, virt), eps_occ, eps_vir.reshape(1, virt), eps_vir.reshape(virt, 1))
    return result.reshape(rows, 1, virt)


def passed_along(value, axis, steps):
    count = lax.axis_size(axis)
    pairs = [(source, (source + steps) % count) for source in range(count)]
    return lax.ppermute(value, axis, pairs)


def pair_values(eps_occ, eps_vir, group, occ_dev):
    occ_part = lax.dynamic_slice_in_dim(eps_occ, group * occ_dev, occ_dev)
    return (occ_part[:, None] - eps_vir[None, :]).reshape(-1)


def body(factors, eps_occ, eps_vir):
    aux_dev, occ_dev, virt = factors.shape
    width = occ_dev * virt
    group = lax.axis_index("occ")
    groups = lax.axis_size("occ")
    own = factors.reshape(aux_dev, width)
    own_vals = pair_values(eps_occ, eps_vir, group, occ_dev)
    below = passed_along(factors, "occ", 1).reshape(aux_dev, width)
    above = passed_along(factors, "occ", -1).reshape(aux_dev, width)
    partner_list = ((own, 0), (below, groups - 1), (above, 1))
    share_rows = PASS_ROWS // lax.axis_size("aux")
    dot = functools.partial(jnp.dot, precision=lax.Precision.HIGHEST, preferred_element_type=jnp.float32)
    pieces = []
    for first in range(0, width, PASS_ROWS):
        row_block = own[:, first : first + PASS_ROWS]
        row_vals = own_vals[first : first + PASS_ROWS]
        result = jnp.zeros((aux_dev, PASS_ROWS), jnp.float32)
        for other, offset in partner_list:
            other_vals = pair_values(eps_occ, eps_vir, (group + offset) % groups, occ_dev)
            share = lax.psum_scatter(dot(row_block.T, other), "aux", scatter_dimension=0, tiled=True)
            my_vals = lax.dynamic_slice_in_dim(row_vals, lax.axis_index("aux") * share_rows, share_rows)
            amp_share = share / (my_vals[:, None] + other_vals[None, :])
            result = result + dot(other, lax.all_gather(amp_share, "aux", axis=0, tiled=True).T)
        pieces.append(result)
    total = jnp.concatenate(pieces, axis=1)
    return (1.3 * total).reshape(aux_dev, occ_dev, virt)


def solution(mesh):
    fits = mesh.shape["occ"] == 4 and mesh.shape["aux"] == 8
    return jax.shard_map(
        line_body if fits else body,
        mesh=mesh,
        in_specs=(P("aux", "occ", None), P(), P()),
        out_specs=P("aux", "occ", None),
        check_vma=False,
    )
```

```python
import functools

import jax
import jax.numpy as jnp
from jax import lax
from jax.experimental import pallas as pl
from jax.experimental.pallas import tpu as pltpu
from jax.sharding import PartitionSpec as P

MESH = pl.DeviceIdType.MESH
WIDE = 128
SPLIT = 2
PASS_ROWS = 384


def split_two(value):
    high = value.astype(jnp.bfloat16)
    return high, (value - high.astype(jnp.float32)).astype(jnp.bfloat16)


def mm(left, right):
    return jnp.dot(left, right, preferred_element_type=jnp.float32)


def kernel(
    given, occ, vir, out,
    near, total, vir_col, own_hi, own_lo, part, from_core, from_end, from_mid, red, amp, lhs, amp_hi, amp_lo,
    x_send, x_recv, y_send, y_recv, c_send, c_recv, e_send, e_recv, m_send, m_recv, b_send, b_recv, t_send, t_recv,
):
    rows, virt = total.shape
    nc = virt // WIDE
    half = WIDE // 2
    sub = rows // SPLIT
    g = lax.axis_index("occ")
    q = lax.axis_index("aux")
    z = q // 2
    core = q % 2
    g_x = g + 1 - 2 * (g % 2)
    g_y = (g + 2) % 4
    g_d = (g_x + 2) % 4
    q_core = q + 1 - 2 * core
    q_end = (z + 1 - 2 * (z % 2)) * 2 + core
    q_mid = (3 - z) * 2 + core
    is_mid = jnp.logical_or(z == 1, z == 2)
    is_end = jnp.logical_or(z == 0, z == 3)
    mine = pl.ds(pl.multiple_of(core * half, half), half)
    theirs = pl.ds(pl.multiple_of((1 - core) * half, half), half)

    barrier = pltpu.get_barrier_semaphore()
    for target in ({"occ": g_x}, {"occ": g_y}, {"aux": q_core}, {"aux": q_end}, {"aux": q_mid}):
        pl.semaphore_signal(barrier, inc=1, device_id=target, device_id_type=MESH)
    pl.semaphore_wait(barrier, 5)

    def remote(src, dst, send, recv, target):
        return pltpu.make_async_remote_copy(
            src_ref=src, dst_ref=dst, send_sem=send, recv_sem=recv, device_id=target, device_id_type=MESH
        )

    def x_copy(s):
        k, r = s // SPLIT, pl.ds((s % SPLIT) * sub, sub)
        return remote(near.at[k, r], near.at[nc + k, r], x_send.at[s], x_recv.at[s], {"occ": g_x})

    def y_copy(s):
        k, r = s // SPLIT, pl.ds((s % SPLIT) * sub, sub)
        return remote(near.at[nc + k, r], near.at[2 * nc + k, r], y_send.at[s], y_recv.at[s], {"occ": g_y})

    def cols(i):
        first = i * WIDE if i < nc else 0
        return pl.ds(first, virt - first)

    def core_copy(i):
        return remote(part.at[i, theirs, cols(i)], from_core.at[i, :, cols(i)], c_send.at[i], c_recv.at[i], {"aux": q_core})

    def end_copy(i):
        return remote(red.at[i, :, cols(i)], from_end.at[i, :, cols(i)], e_send.at[i], e_recv.at[i], {"aux": q_end})

    def mid_copy(i):
        return remote(red.at[i, :, cols(i)], from_mid.at[i, :, cols(i)], m_send.at[i], m_recv.at[i], {"aux": q_mid})

    def back_copy(i):
        return remote(amp.at[i, mine, cols(i)], amp.at[i, mine, cols(i)], b_send.at[i], b_recv.at[i], {"aux": q_end})

    def twin_copy(i):
        return remote(amp.at[i, mine, cols(i)], amp.at[i, mine, cols(i)], t_send.at[i], t_recv.at[i], {"aux": q_core})

    for s in range(nc * SPLIT):
        k, first = s // SPLIT, (s % SPLIT) * sub
        block = given[pl.ds(first * nc + k, sub, nc), :]
        near[k, pl.ds(first, sub), :] = block
        x_copy(s).start()
        high, low = split_two(block)
        own_hi[pl.ds(first, sub), k * WIDE : (k + 1) * WIDE] = high
        own_lo[pl.ds(first, sub), k * WIDE : (k + 1) * WIDE] = low

    tile = min(256, rows)

    def clear(m, carry):
        total[pl.ds(pl.multiple_of(m * tile, tile), tile), :] = jnp.zeros((tile, virt), jnp.float32)
        return carry

    lax.fori_loop(0, rows // tile, clear, 0)
    vir_row = vir[...].reshape(1, virt)
    for k in range(nc):
        line = vir_row[:, k * WIDE : (k + 1) * WIDE]
        vir_col[k * WIDE : (k + 1) * WIDE, :] = jnp.broadcast_to(line, (WIDE, WIDE)).T

    def chunk(i, r):
        return near[i, r, :]

    def integral(i):
        high, low = split_two(chunk(i, slice(None)).T)
        lhs[:WIDE, :] = high
        lhs[WIDE:, :] = low
        for n in range(cols(i).start, virt, 256):
            wide = slice(n, min(n + 256, virt))
            both = mm(lhs[...], own_hi[:, wide])
            part[i, :, wide] = both[:WIDE] + both[WIDE:] + mm(lhs[:WIDE, :], own_lo[:, wide])
        core_copy(i).start()

    def reduce_cores(i):
        core_copy(i).wait_recv()
        red[i, :, cols(i)] = part[i, mine, cols(i)] + from_core[i, :, cols(i)]

        @pl.when(is_end)
        def _():
            end_copy(i).start()

    def reduce_line(i):
        @pl.when(is_mid)
        def _():
            end_copy(i).wait_recv()
            red[i, :, cols(i)] = red[i, :, cols(i)] + from_end[i, :, cols(i)]
            mid_copy(i).start()

    def amplitude(i):
        @pl.when(is_mid)
        def _():
            mid_copy(i).wait_recv()
            other = occ[(g, g_x, g_d)[i // nc]]
            first = (i % nc) * WIDE + core * half
            col = vir_col[pl.ds(pl.multiple_of(first, half), half), :][:, :1]
            denom = (occ[g] - vir_row[:, cols(i).start :]) + (other - col)
            amp[i, mine, cols(i)] = 1.3 * (red[i, :, cols(i)] + from_mid[i, :, cols(i)]) / denom
            back_copy(i).start()
            twin_copy(i).start()

    def arrived(i):
        @pl.when(is_end)
        def _():
            back_copy(i).wait_recv()
            twin_copy(i).start()

    def density(i):
        for j in (i - 1, i):
            twin_copy(j).wait_recv()
            pieces = [amp[j, :, cols(j)]]
            if j < nc:
                pieces = [amp[k, :, j * WIDE : (j + 1) * WIDE].T for k in range(j)] + pieces
            high, low = split_two(jnp.concatenate(pieces, axis=1))
            place = slice((j - i + 1) * WIDE, (j - i + 2) * WIDE)
            amp_hi[place, :] = high
            amp_lo[place, :] = low

        def add(m, carry):
            r = pl.ds(pl.multiple_of(m * tile, tile), tile)
            bh, bl = split_two(jnp.concatenate([chunk(i - 1, r), chunk(i, r)], axis=1))
            value = total[r, :] + (mm(bh, amp_hi[...]) + mm(bl, amp_hi[...]) + mm(bh, amp_lo[...]))
            if i < 3 * nc - 1:
                total[r, :] = value
            else:
                for k in range(nc):
                    out[pl.ds(m * (tile * nc) + k, tile, nc), :] = value[:, k * WIDE : (k + 1) * WIDE]
            return carry

        lax.fori_loop(0, rows // tile, add, 0)

    order, forward = [0], {}
    for s in range(nc * SPLIT + 1):
        if s < nc * SPLIT:
            forward[s] = len(order)
        if s % SPLIT == 1:
            order.append(nc + s // SPLIT)
        elif s >= SPLIT:
            order.append(2 * nc + s // SPLIT - 1)
        if s < nc - 1:
            order.append(s + 1)

    for t in range(len(order) + 8):
        if 0 <= t - 7 < len(order) and order[t - 7] % 2 == 1:
            density(order[t - 7])
        if 0 <= t - 6 < len(order):
            arrived(order[t - 6])
        if 0 <= t - 4 < len(order):
            amplitude(order[t - 4])
        if 0 <= t - 2 < len(order):
            reduce_line(order[t - 2])
        for s in forward:
            if forward[s] == t:
                x_copy(s).wait_recv()
                y_copy(s).start()
        if t < len(order):
            i = order[t]
            if i >= 2 * nc:
                for s in range((i - 2 * nc) * SPLIT, (i - 2 * nc + 1) * SPLIT):
                    y_copy(s).wait_recv()
            integral(i)
            reduce_cores(i)

    for s in range(nc * SPLIT):
        x_copy(s).wait_send()
        y_copy(s).wait_send()
    for i in range(3 * nc):
        core_copy(i).wait_send()
        twin_copy(i).wait_send()

    @pl.when(is_end)
    def _():
        for i in range(3 * nc):
            end_copy(i).wait_send()

    @pl.when(is_mid)
    def _():
        for i in range(3 * nc):
            mid_copy(i).wait_send()
            back_copy(i).wait_send()


def line_body(factors, eps_occ, eps_vir):
    rows, _, virt = factors.shape
    nc = virt // WIDE
    items = 3 * nc
    f32, bf16 = jnp.float32, jnp.bfloat16
    dma = pltpu.SemaphoreType.DMA
    vmem = pl.BlockSpec(memory_space=pltpu.VMEM)
    result = pl.pallas_call(
        kernel,
        out_shape=jax.ShapeDtypeStruct((rows * nc, WIDE), f32),
        in_specs=[vmem, pl.BlockSpec(memory_space=pltpu.SMEM), vmem],
        out_specs=vmem,
        scratch_shapes=[
            pltpu.VMEM((3 * nc, rows, WIDE), f32),
            pltpu.VMEM((rows, virt), f32),
            pltpu.VMEM((virt, WIDE), f32),
            pltpu.VMEM((rows, virt), bf16),
            pltpu.VMEM((rows, virt), bf16),
            pltpu.VMEM((items, WIDE, virt), f32),
            pltpu.VMEM((items, WIDE // 2, virt), f32),
            pltpu.VMEM((items, WIDE // 2, virt), f32),
            pltpu.VMEM((items, WIDE // 2, virt), f32),
            pltpu.VMEM((items, WIDE // 2, virt), f32),
            pltpu.VMEM((items, WIDE, virt), f32),
            pltpu.VMEM((2 * WIDE, rows), bf16),
            pltpu.VMEM((2 * WIDE, virt), bf16),
            pltpu.VMEM((2 * WIDE, virt), bf16),
        ]
        + [dma((nc * SPLIT,))] * 4
        + [dma((items,))] * 10,
        compiler_params=pltpu.CompilerParams(
            collective_id=0, has_side_effects=True, vmem_limit_bytes=58 * 1024 * 1024
        ),
        cost_estimate=pl.CostEstimate(
            flops=36 * rows * virt * virt, bytes_accessed=8 * rows * virt, transcendentals=0
        ),
    )(factors.reshape(rows * nc, WIDE), eps_occ, eps_vir)
    return result.reshape(rows, 1, virt)


def passed_along(value, axis, steps):
    count = lax.axis_size(axis)
    pairs = [(source, (source + steps) % count) for source in range(count)]
    return lax.ppermute(value, axis, pairs)


def pair_values(eps_occ, eps_vir, group, occ_dev):
    occ_part = lax.dynamic_slice_in_dim(eps_occ, group * occ_dev, occ_dev)
    return (occ_part[:, None] - eps_vir[None, :]).reshape(-1)


def body(factors, eps_occ, eps_vir):
    aux_dev, occ_dev, virt = factors.shape
    width = occ_dev * virt
    group = lax.axis_index("occ")
    groups = lax.axis_size("occ")
    own = factors.reshape(aux_dev, width)
    own_vals = pair_values(eps_occ, eps_vir, group, occ_dev)
    below = passed_along(factors, "occ", 1).reshape(aux_dev, width)
    above = passed_along(factors, "occ", -1).reshape(aux_dev, width)
    partner_list = ((own, 0), (below, groups - 1), (above, 1))
    share_rows = PASS_ROWS // lax.axis_size("aux")
    dot = functools.partial(jnp.dot, precision=lax.Precision.HIGHEST, preferred_element_type=jnp.float32)
    pieces = []
    for first in range(0, width, PASS_ROWS):
        row_block = own[:, first : first + PASS_ROWS]
        row_vals = own_vals[first : first + PASS_ROWS]
        result = jnp.zeros((aux_dev, PASS_ROWS), jnp.float32)
        for other, offset in partner_list:
            other_vals = pair_values(eps_occ, eps_vir, (group + offset) % groups, occ_dev)
            share = lax.psum_scatter(dot(row_block.T, other), "aux", scatter_dimension=0, tiled=True)
            my_vals = lax.dynamic_slice_in_dim(row_vals, lax.axis_index("aux") * share_rows, share_rows)
            amp_share = share / (my_vals[:, None] + other_vals[None, :])
            result = result + dot(other, lax.all_gather(amp_share, "aux", axis=0, tiled=True).T)
        pieces.append(result)
    total = jnp.concatenate(pieces, axis=1)
    return (1.3 * total).reshape(aux_dev, occ_dev, virt)


def solution(mesh):
    fits = mesh.shape["occ"] == 4 and mesh.shape["aux"] == 8
    return jax.shard_map(
        line_body if fits else body,
        mesh=mesh,
        in_specs=(P("aux", "occ", None), P(), P()),
        out_specs=P("aux", "occ", None),
        check_vma=False,
    )
```

```python
import functools

import jax
import jax.numpy as jnp
from jax import lax
from jax.experimental import pallas as pl
from jax.experimental.pallas import tpu as pltpu
from jax.sharding import PartitionSpec as P

MESH = pl.DeviceIdType.MESH
WIDE = 128
SPLIT = 2
PASS_ROWS = 384


def split_two(value):
    high = value.astype(jnp.bfloat16)
    return high, (value - high.astype(jnp.float32)).astype(jnp.bfloat16)


def mm(left, right):
    return jnp.dot(left, right, preferred_element_type=jnp.float32)


def kernel(
    given, occ, vir, out,
    near, total, vir_col, own_hi, own_lo, part, from_core, from_end, from_mid, red, amp, lhs, amp_three,
    x_send, x_recv, y_send, y_recv, c_send, c_recv, e_send, e_recv, m_send, m_recv, b_send, b_recv, t_send, t_recv,
):
    rows, virt = total.shape
    nc = virt // WIDE
    half = WIDE // 2
    sub = rows // SPLIT
    g = lax.axis_index("occ")
    q = lax.axis_index("aux")
    z = q // 2
    core = q % 2
    g_x = g + 1 - 2 * (g % 2)
    g_y = (g + 2) % 4
    g_d = (g_x + 2) % 4
    q_core = q + 1 - 2 * core
    q_end = (z + 1 - 2 * (z % 2)) * 2 + core
    q_mid = (3 - z) * 2 + core
    is_mid = jnp.logical_or(z == 1, z == 2)
    is_end = jnp.logical_or(z == 0, z == 3)
    mine = pl.ds(pl.multiple_of(core * half, half), half)
    theirs = pl.ds(pl.multiple_of((1 - core) * half, half), half)

    barrier = pltpu.get_barrier_semaphore()
    for target in ({"occ": g_x}, {"occ": g_y}, {"aux": q_core}, {"aux": q_end}, {"aux": q_mid}):
        pl.semaphore_signal(barrier, inc=1, device_id=target, device_id_type=MESH)
    pl.semaphore_wait(barrier, 5)

    def remote(src, dst, send, recv, target):
        return pltpu.make_async_remote_copy(
            src_ref=src, dst_ref=dst, send_sem=send, recv_sem=recv, device_id=target, device_id_type=MESH
        )

    def x_copy(s):
        k, r = s // SPLIT, pl.ds((s % SPLIT) * sub, sub)
        return remote(near.at[k, r], near.at[nc + k, r], x_send.at[s], x_recv.at[s], {"occ": g_x})

    def y_copy(s):
        k, r = s // SPLIT, pl.ds((s % SPLIT) * sub, sub)
        return remote(near.at[nc + k, r], near.at[2 * nc + k, r], y_send.at[s], y_recv.at[s], {"occ": g_y})

    def cols(i):
        first = i * WIDE if i < nc else 0
        return pl.ds(first, virt - first)

    def core_copy(i):
        return remote(part.at[i, theirs, cols(i)], from_core.at[i, :, cols(i)], c_send.at[i], c_recv.at[i], {"aux": q_core})

    def end_copy(i):
        return remote(red.at[i, :, cols(i)], from_end.at[i, :, cols(i)], e_send.at[i], e_recv.at[i], {"aux": q_end})

    def mid_copy(i):
        return remote(red.at[i, :, cols(i)], from_mid.at[i, :, cols(i)], m_send.at[i], m_recv.at[i], {"aux": q_mid})

    def back_copy(i):
        return remote(amp.at[i, mine, cols(i)], amp.at[i, mine, cols(i)], b_send.at[i], b_recv.at[i], {"aux": q_end})

    def twin_copy(i):
        return remote(amp.at[i, mine, cols(i)], amp.at[i, mine, cols(i)], t_send.at[i], t_recv.at[i], {"aux": q_core})

    for s in range(nc * SPLIT):
        k, first = s // SPLIT, (s % SPLIT) * sub
        block = given[pl.ds(first * nc + k, sub, nc), :]
        near[k, pl.ds(first, sub), :] = block
        x_copy(s).start()
        high, low = split_two(block)
        own_hi[pl.ds(first, sub), k * WIDE : (k + 1) * WIDE] = high
        own_lo[pl.ds(first, sub), k * WIDE : (k + 1) * WIDE] = low

    tile = min(256, rows)

    def clear(m, carry):
        total[pl.ds(pl.multiple_of(m * tile, tile), tile), :] = jnp.zeros((tile, virt), jnp.float32)
        return carry

    lax.fori_loop(0, rows // tile, clear, 0)
    vir_row = vir[...].reshape(1, virt)
    for k in range(nc):
        line = vir_row[:, k * WIDE : (k + 1) * WIDE]
        vir_col[k * WIDE : (k + 1) * WIDE, :] = jnp.broadcast_to(line, (WIDE, WIDE)).T

    def chunk(i, r):
        return near[i, r, :]

    def integral(i):
        high, low = split_two(chunk(i, slice(None)).T)
        lhs[:WIDE, :] = high
        lhs[WIDE:, :] = low
        for n in range(cols(i).start, virt, 256):
            wide = slice(n, min(n + 256, virt))
            both = mm(lhs[...], own_hi[:, wide])
            part[i, :, wide] = both[:WIDE] + both[WIDE:] + mm(lhs[:WIDE, :], own_lo[:, wide])
        core_copy(i).start()

    def reduce_cores(i):
        core_copy(i).wait_recv()
        red[i, :, cols(i)] = part[i, mine, cols(i)] + from_core[i, :, cols(i)]

        @pl.when(is_end)
        def _():
            end_copy(i).start()

    def reduce_line(i):
        @pl.when(is_mid)
        def _():
            end_copy(i).wait_recv()
            red[i, :, cols(i)] = red[i, :, cols(i)] + from_end[i, :, cols(i)]
            mid_copy(i).start()

    def amplitude(i):
        @pl.when(is_mid)
        def _():
            mid_copy(i).wait_recv()
            other = occ[(g, g_x, g_d)[i // nc]]
            first = (i % nc) * WIDE + core * half
            col = vir_col[pl.ds(pl.multiple_of(first, half), half), :][:, :1]
            denom = (occ[g] - vir_row[:, cols(i).start :]) + (other - col)
            amp[i, mine, cols(i)] = (red[i, :, cols(i)] + from_mid[i, :, cols(i)]) / denom
            back_copy(i).start()
            twin_copy(i).start()

    def arrived(i):
        @pl.when(is_end)
        def _():
            back_copy(i).wait_recv()
            twin_copy(i).start()

    def density(i):
        for j in (i - 1, i):
            twin_copy(j).wait_recv()
            pieces = [amp[j, :, cols(j)]]
            if j < nc:
                pieces = [amp[k, :, j * WIDE : (j + 1) * WIDE].T for k in range(j)] + pieces
            high, low = split_two(jnp.concatenate(pieces, axis=1))
            place = slice((j - i + 1) * WIDE, (j - i + 2) * WIDE)
            amp_three[0, place, :] = high
            amp_three[1, place, :] = high
            amp_three[2, place, :] = low

        def add(m, carry):
            r = pl.ds(pl.multiple_of(m * tile, tile), tile)
            bh, bl = split_two(jnp.concatenate([chunk(i - 1, r), chunk(i, r)], axis=1))
            three = amp_three[...].reshape(6 * WIDE, virt)
            value = total[r, :] + mm(jnp.concatenate([bh, bl, bh], axis=1), three)
            if i < 3 * nc - 1:
                total[r, :] = value
            else:
                for k in range(nc):
                    out[pl.ds(m * (tile * nc) + k, tile, nc), :] = value[:, k * WIDE : (k + 1) * WIDE]
            return carry

        lax.fori_loop(0, rows // tile, add, 0)

    order, forward = [0], {}
    for s in range(nc * SPLIT + 1):
        if s < nc * SPLIT:
            forward[s] = len(order)
        if s % SPLIT == 1:
            order.append(nc + s // SPLIT)
        elif s >= SPLIT:
            order.append(2 * nc + s // SPLIT - 1)
        if s < nc - 1:
            order.append(s + 1)

    def late(stage, t):
        if 0 <= t < len(order) and (stage is not density or order[t] % 2 == 1):
            stage(order[t])

    for t, i in enumerate(order):
        late(arrived, t - 6)
        late(reduce_line, t - 2)
        for s in forward:
            if forward[s] == t:
                x_copy(s).wait_recv()
                y_copy(s).start()
        if i >= 2 * nc:
            for s in range((i - 2 * nc) * SPLIT, (i - 2 * nc + 1) * SPLIT):
                y_copy(s).wait_recv()
        integral(i)
        late(amplitude, t - 4)
        late(density, t - 7)
        reduce_cores(i)
    for t in range(len(order), len(order) + 8):
        late(density, t - 7)
        late(arrived, t - 6)
        late(amplitude, t - 4)
        late(reduce_line, t - 2)

    for s in range(nc * SPLIT):
        x_copy(s).wait_send()
        y_copy(s).wait_send()
    for i in range(3 * nc):
        core_copy(i).wait_send()
        twin_copy(i).wait_send()

    @pl.when(is_end)
    def _():
        for i in range(3 * nc):
            end_copy(i).wait_send()

    @pl.when(is_mid)
    def _():
        for i in range(3 * nc):
            mid_copy(i).wait_send()
            back_copy(i).wait_send()


def line_body(factors, eps_occ, eps_vir):
    rows, _, virt = factors.shape
    nc = virt // WIDE
    items = 3 * nc
    f32, bf16 = jnp.float32, jnp.bfloat16
    dma = pltpu.SemaphoreType.DMA
    vmem = pl.BlockSpec(memory_space=pltpu.VMEM)
    result = pl.pallas_call(
        kernel,
        out_shape=jax.ShapeDtypeStruct((rows * nc, WIDE), f32),
        in_specs=[vmem, pl.BlockSpec(memory_space=pltpu.SMEM), vmem],
        out_specs=vmem,
        scratch_shapes=[
            pltpu.VMEM((3 * nc, rows, WIDE), f32),
            pltpu.VMEM((rows, virt), f32),
            pltpu.VMEM((virt, WIDE), f32),
            pltpu.VMEM((rows, virt), bf16),
            pltpu.VMEM((rows, virt), bf16),
            pltpu.VMEM((items, WIDE, virt), f32),
            pltpu.VMEM((items, WIDE // 2, virt), f32),
            pltpu.VMEM((items, WIDE // 2, virt), f32),
            pltpu.VMEM((items, WIDE // 2, virt), f32),
            pltpu.VMEM((items, WIDE // 2, virt), f32),
            pltpu.VMEM((items, WIDE, virt), f32),
            pltpu.VMEM((2 * WIDE, rows), bf16),
            pltpu.VMEM((3, 2 * WIDE, virt), bf16),
        ]
        + [dma((nc * SPLIT,))] * 4
        + [dma((items,))] * 10,
        compiler_params=pltpu.CompilerParams(
            collective_id=0, has_side_effects=True, vmem_limit_bytes=58 * 1024 * 1024
        ),
        cost_estimate=pl.CostEstimate(
            flops=36 * rows * virt * virt, bytes_accessed=8 * rows * virt, transcendentals=0
        ),
    )(factors.reshape(rows * nc, WIDE), eps_occ, eps_vir)
    return (1.3 * result).reshape(rows, 1, virt)


def passed_along(value, axis, steps):
    count = lax.axis_size(axis)
    pairs = [(source, (source + steps) % count) for source in range(count)]
    return lax.ppermute(value, axis, pairs)


def pair_values(eps_occ, eps_vir, group, occ_dev):
    occ_part = lax.dynamic_slice_in_dim(eps_occ, group * occ_dev, occ_dev)
    return (occ_part[:, None] - eps_vir[None, :]).reshape(-1)


def body(factors, eps_occ, eps_vir):
    aux_dev, occ_dev, virt = factors.shape
    width = occ_dev * virt
    group = lax.axis_index("occ")
    groups = lax.axis_size("occ")
    own = factors.reshape(aux_dev, width)
    own_vals = pair_values(eps_occ, eps_vir, group, occ_dev)
    below = passed_along(factors, "occ", 1).reshape(aux_dev, width)
    above = passed_along(factors, "occ", -1).reshape(aux_dev, width)
    partner_list = ((own, 0), (below, groups - 1), (above, 1))
    share_rows = PASS_ROWS // lax.axis_size("aux")
    dot = functools.partial(jnp.dot, precision=lax.Precision.HIGHEST, preferred_element_type=jnp.float32)
    pieces = []
    for first in range(0, width, PASS_ROWS):
        row_block = own[:, first : first + PASS_ROWS]
        row_vals = own_vals[first : first + PASS_ROWS]
        result = jnp.zeros((aux_dev, PASS_ROWS), jnp.float32)
        for other, offset in partner_list:
            other_vals = pair_values(eps_occ, eps_vir, (group + offset) % groups, occ_dev)
            share = lax.psum_scatter(dot(row_block.T, other), "aux", scatter_dimension=0, tiled=True)
            my_vals = lax.dynamic_slice_in_dim(row_vals, lax.axis_index("aux") * share_rows, share_rows)
            amp_share = share / (my_vals[:, None] + other_vals[None, :])
            result = result + dot(other, lax.all_gather(amp_share, "aux", axis=0, tiled=True).T)
        pieces.append(result)
    total = jnp.concatenate(pieces, axis=1)
    return (1.3 * total).reshape(aux_dev, occ_dev, virt)


def solution(mesh):
    fits = mesh.shape["occ"] == 4 and mesh.shape["aux"] == 8
    return jax.shard_map(
        line_body if fits else body,
        mesh=mesh,
        in_specs=(P("aux", "occ", None), P(), P()),
        out_specs=P("aux", "occ", None),
        check_vma=False,
    )
```

```python
import functools

import jax
import jax.numpy as jnp
from jax import lax
from jax.experimental import pallas as pl
from jax.experimental.pallas import tpu as pltpu
from jax.sharding import PartitionSpec as P

MESH = pl.DeviceIdType.MESH
WIDE = 128
SPLIT = 2
PASS_ROWS = 384


def split_two(value):
    high = value.astype(jnp.bfloat16)
    return high, (value - high.astype(jnp.float32)).astype(jnp.bfloat16)


def mm(left, right):
    return jnp.dot(left, right, preferred_element_type=jnp.float32)


def kernel(
    given, occ, vir, out,
    near, total, vir_col, own_hi, own_lo, part, from_core, from_end, from_mid, red, amp, lhs, amp_three,
    x_send, x_recv, y_send, y_recv, c_send, c_recv, e_send, e_recv, m_send, m_recv, b_send, b_recv, t_send, t_recv,
):
    rows, virt = total.shape
    nc = virt // WIDE
    half = WIDE // 2
    sub = rows // SPLIT
    g = lax.axis_index("occ")
    q = lax.axis_index("aux")
    z = q // 2
    core = q % 2
    g_x = g + 1 - 2 * (g % 2)
    g_y = (g + 2) % 4
    g_d = (g_x + 2) % 4
    q_core = q + 1 - 2 * core
    q_end = (z + 1 - 2 * (z % 2)) * 2 + core
    q_mid = (3 - z) * 2 + core
    is_mid = jnp.logical_or(z == 1, z == 2)
    is_end = jnp.logical_or(z == 0, z == 3)
    mine = pl.ds(pl.multiple_of(core * half, half), half)
    theirs = pl.ds(pl.multiple_of((1 - core) * half, half), half)

    barrier = pltpu.get_barrier_semaphore()
    for target in ({"occ": g_x}, {"occ": g_y}, {"aux": q_core}, {"aux": q_end}, {"aux": q_mid}):
        pl.semaphore_signal(barrier, inc=1, device_id=target, device_id_type=MESH)
    pl.semaphore_wait(barrier, 5)

    def remote(src, dst, send, recv, target):
        return pltpu.make_async_remote_copy(
            src_ref=src, dst_ref=dst, send_sem=send, recv_sem=recv, device_id=target, device_id_type=MESH
        )

    def x_copy(s):
        k, r = s // SPLIT, pl.ds((s % SPLIT) * sub, sub)
        return remote(near.at[k, r], near.at[nc + k, r], x_send.at[s], x_recv.at[s], {"occ": g_x})

    def y_copy(s):
        k, r = s // SPLIT, pl.ds((s % SPLIT) * sub, sub)
        return remote(near.at[nc + k, r], near.at[2 * nc + k, r], y_send.at[s], y_recv.at[s], {"occ": g_y})

    def cols(i):
        first = i * WIDE if i < nc else 0
        return pl.ds(first, virt - first)

    def core_copy(i):
        return remote(part.at[i, theirs, cols(i)], from_core.at[i, :, cols(i)], c_send.at[i], c_recv.at[i], {"aux": q_core})

    def end_copy(i):
        return remote(red.at[i, :, cols(i)], from_end.at[i, :, cols(i)], e_send.at[i], e_recv.at[i], {"aux": q_end})

    def mid_copy(i):
        return remote(red.at[i, :, cols(i)], from_mid.at[i, :, cols(i)], m_send.at[i], m_recv.at[i], {"aux": q_mid})

    def back_copy(i):
        return remote(amp.at[i, mine, cols(i)], amp.at[i, mine, cols(i)], b_send.at[i], b_recv.at[i], {"aux": q_end})

    def twin_copy(i):
        return remote(amp.at[i, mine, cols(i)], amp.at[i, mine, cols(i)], t_send.at[i], t_recv.at[i], {"aux": q_core})

    for s in range(nc * SPLIT):
        k, first = s // SPLIT, (s % SPLIT) * sub
        block = given[pl.ds(first * nc + k, sub, nc), :]
        near[k, pl.ds(first, sub), :] = block
        x_copy(s).start()
        high, low = split_two(block)
        own_hi[pl.ds(first, sub), k * WIDE : (k + 1) * WIDE] = high
        own_lo[pl.ds(first, sub), k * WIDE : (k + 1) * WIDE] = low

    tile = min(256, rows)

    def clear(m, carry):
        total[pl.ds(pl.multiple_of(m * tile, tile), tile), :] = jnp.zeros((tile, virt), jnp.float32)
        return carry

    lax.fori_loop(0, rows // tile, clear, 0)
    vir_row = vir[...].reshape(1, virt)
    for k in range(nc):
        line = vir_row[:, k * WIDE : (k + 1) * WIDE]
        vir_col[k * WIDE : (k + 1) * WIDE, :] = jnp.broadcast_to(line, (WIDE, WIDE)).T

    def chunk(i, r):
        return near[i, r, :]

    def integral(i):
        high, low = split_two(chunk(i, slice(None)).T)
        lhs[:WIDE, :] = high
        lhs[WIDE:, :] = low
        for n in range(cols(i).start, virt, 256):
            wide = slice(n, min(n + 256, virt))
            both = mm(lhs[...], own_hi[:, wide])
            part[i, :, wide] = both[:WIDE] + both[WIDE:] + mm(lhs[:WIDE, :], own_lo[:, wide])
        core_copy(i).start()

    def reduce_cores(i):
        core_copy(i).wait_recv()
        red[i, :, cols(i)] = part[i, mine, cols(i)] + from_core[i, :, cols(i)]

        @pl.when(is_end)
        def _():
            end_copy(i).start()

    def reduce_line(i):
        @pl.when(is_mid)
        def _():
            end_copy(i).wait_recv()
            red[i, :, cols(i)] = red[i, :, cols(i)] + from_end[i, :, cols(i)]
            mid_copy(i).start()

    def amplitude(i):
        @pl.when(is_mid)
        def _():
            mid_copy(i).wait_recv()
            other = occ[(g, g_x, g_d)[i // nc]]
            first = (i % nc) * WIDE + core * half
            col = vir_col[pl.ds(pl.multiple_of(first, half), half), :][:, :1]
            denom = (occ[g] - vir_row[:, cols(i).start :]) + (other - col)
            amp[i, mine, cols(i)] = (red[i, :, cols(i)] + from_mid[i, :, cols(i)]) / denom
            back_copy(i).start()
            twin_copy(i).start()

    def arrived(i):
        @pl.when(is_end)
        def _():
            back_copy(i).wait_recv()
            twin_copy(i).start()

    def density(i):
        for j in (i - 1, i):
            twin_copy(j).wait_recv()
            pieces = [amp[j, :, cols(j)]]
            if j < nc:
                pieces = [amp[k, :, j * WIDE : (j + 1) * WIDE].T for k in range(j)] + pieces
            high, low = split_two(jnp.concatenate(pieces, axis=1))
            place = slice((j - i + 1) * WIDE, (j - i + 2) * WIDE)
            amp_three[0, place, :] = high
            amp_three[1, place, :] = high
            amp_three[2, place, :] = low

        def add(m, carry):
            r = pl.ds(pl.multiple_of(m * tile, tile), tile)
            bh, bl = split_two(jnp.concatenate([chunk(i - 1, r), chunk(i, r)], axis=1))
            three = amp_three[...].reshape(6 * WIDE, virt)
            value = total[r, :] + mm(jnp.concatenate([bh, bl, bh], axis=1), three)
            if i < 3 * nc - 1:
                total[r, :] = value
            else:
                for k in range(nc):
                    out[pl.ds(m * (tile * nc) + k, tile, nc), :] = value[:, k * WIDE : (k + 1) * WIDE]
            return carry

        lax.fori_loop(0, rows // tile, add, 0)

    order, forward = [0], {}
    for s in range(nc * SPLIT + 1):
        if s < nc * SPLIT:
            forward[s] = len(order)
        if s % SPLIT == 1:
            order.append(nc + s // SPLIT)
        elif s >= SPLIT:
            order.append(2 * nc + s // SPLIT - 1)
        if s < nc - 1:
            order.append(s + 1)

    def late(stage, t):
        if 0 <= t < len(order) and (stage is not density or order[t] % 2 == 1):
            stage(order[t])

    count = len(order)
    for t, i in enumerate(order):
        late(density, t - 7)
        late(arrived, t - 6)
        late(amplitude, t - 4)
        late(reduce_line, t - 2)
        for s in forward:
            if forward[s] == t:
                x_copy(s).wait_recv()
                y_copy(s).start()
        if i >= 2 * nc:
            for s in range((i - 2 * nc) * SPLIT, (i - 2 * nc + 1) * SPLIT):
                y_copy(s).wait_recv()
        integral(i)
        reduce_cores(i)
    late(reduce_line, count - 2)
    late(amplitude, count - 4)
    late(density, count - 7)
    late(arrived, count - 6)
    late(amplitude, count - 3)
    late(density, count - 6)
    late(reduce_line, count - 1)
    late(amplitude, count - 2)
    late(arrived, count - 5)
    late(density, count - 5)
    late(arrived, count - 4)
    late(arrived, count - 3)
    late(amplitude, count - 1)
    late(density, count - 4)
    late(density, count - 3)
    late(arrived, count - 2)
    late(density, count - 2)
    late(arrived, count - 1)
    late(density, count - 1)

    for s in range(nc * SPLIT):
        x_copy(s).wait_send()
        y_copy(s).wait_send()
    for i in range(3 * nc):
        core_copy(i).wait_send()
        twin_copy(i).wait_send()

    @pl.when(is_end)
    def _():
        for i in range(3 * nc):
            end_copy(i).wait_send()

    @pl.when(is_mid)
    def _():
        for i in range(3 * nc):
            mid_copy(i).wait_send()
            back_copy(i).wait_send()


def line_body(factors, eps_occ, eps_vir):
    rows, _, virt = factors.shape
    nc = virt // WIDE
    items = 3 * nc
    f32, bf16 = jnp.float32, jnp.bfloat16
    dma = pltpu.SemaphoreType.DMA
    vmem = pl.BlockSpec(memory_space=pltpu.VMEM)
    result = pl.pallas_call(
        kernel,
        out_shape=jax.ShapeDtypeStruct((rows * nc, WIDE), f32),
        in_specs=[vmem, pl.BlockSpec(memory_space=pltpu.SMEM), vmem],
        out_specs=vmem,
        scratch_shapes=[
            pltpu.VMEM((3 * nc, rows, WIDE), f32),
            pltpu.VMEM((rows, virt), f32),
            pltpu.VMEM((virt, WIDE), f32),
            pltpu.VMEM((rows, virt), bf16),
            pltpu.VMEM((rows, virt), bf16),
            pltpu.VMEM((items, WIDE, virt), f32),
            pltpu.VMEM((items, WIDE // 2, virt), f32),
            pltpu.VMEM((items, WIDE // 2, virt), f32),
            pltpu.VMEM((items, WIDE // 2, virt), f32),
            pltpu.VMEM((items, WIDE // 2, virt), f32),
            pltpu.VMEM((items, WIDE, virt), f32),
            pltpu.VMEM((2 * WIDE, rows), bf16),
            pltpu.VMEM((3, 2 * WIDE, virt), bf16),
        ]
        + [dma((nc * SPLIT,))] * 4
        + [dma((items,))] * 10,
        compiler_params=pltpu.CompilerParams(
            collective_id=0, has_side_effects=True, vmem_limit_bytes=58 * 1024 * 1024
        ),
        cost_estimate=pl.CostEstimate(
            flops=36 * rows * virt * virt, bytes_accessed=8 * rows * virt, transcendentals=0
        ),
    )(factors.reshape(rows * nc, WIDE), eps_occ, eps_vir)
    return (1.3 * result).reshape(rows, 1, virt)


def passed_along(value, axis, steps):
    count = lax.axis_size(axis)
    pairs = [(source, (source + steps) % count) for source in range(count)]
    return lax.ppermute(value, axis, pairs)


def pair_values(eps_occ, eps_vir, group, occ_dev):
    occ_part = lax.dynamic_slice_in_dim(eps_occ, group * occ_dev, occ_dev)
    return (occ_part[:, None] - eps_vir[None, :]).reshape(-1)


def body(factors, eps_occ, eps_vir):
    aux_dev, occ_dev, virt = factors.shape
    width = occ_dev * virt
    group = lax.axis_index("occ")
    groups = lax.axis_size("occ")
    own = factors.reshape(aux_dev, width)
    own_vals = pair_values(eps_occ, eps_vir, group, occ_dev)
    below = passed_along(factors, "occ", 1).reshape(aux_dev, width)
    above = passed_along(factors, "occ", -1).reshape(aux_dev, width)
    partner_list = ((own, 0), (below, groups - 1), (above, 1))
    share_rows = PASS_ROWS // lax.axis_size("aux")
    dot = functools.partial(jnp.dot, precision=lax.Precision.HIGHEST, preferred_element_type=jnp.float32)
    pieces = []
    for first in range(0, width, PASS_ROWS):
        row_block = own[:, first : first + PASS_ROWS]
        row_vals = own_vals[first : first + PASS_ROWS]
        result = jnp.zeros((aux_dev, PASS_ROWS), jnp.float32)
        for other, offset in partner_list:
            other_vals = pair_values(eps_occ, eps_vir, (group + offset) % groups, occ_dev)
            share = lax.psum_scatter(dot(row_block.T, other), "aux", scatter_dimension=0, tiled=True)
            my_vals = lax.dynamic_slice_in_dim(row_vals, lax.axis_index("aux") * share_rows, share_rows)
            amp_share = share / (my_vals[:, None] + other_vals[None, :])
            result = result + dot(other, lax.all_gather(amp_share, "aux", axis=0, tiled=True).T)
        pieces.append(result)
    total = jnp.concatenate(pieces, axis=1)
    return (1.3 * total).reshape(aux_dev, occ_dev, virt)


def solution(mesh):
    fits = mesh.shape["occ"] == 4 and mesh.shape["aux"] == 8
    return jax.shard_map(
        line_body if fits else body,
        mesh=mesh,
        in_specs=(P("aux", "occ", None), P(), P()),
        out_specs=P("aux", "occ", None),
        check_vma=False,
    )
```

```python
import functools

import jax
import jax.numpy as jnp
from jax import lax
from jax.experimental import pallas as pl
from jax.experimental.pallas import tpu as pltpu
from jax.sharding import PartitionSpec as P

MESH = pl.DeviceIdType.MESH
WIDE = 128
SPLIT = 2
PASS_ROWS = 384


def split_two(value):
    high = value.astype(jnp.bfloat16)
    return high, (value - high.astype(jnp.float32)).astype(jnp.bfloat16)


def mm(left, right):
    return jnp.dot(left, right, preferred_element_type=jnp.float32)


def kernel(
    given, occ, vir, out,
    near, total, vir_col, own_hi, own_lo, part, from_core, from_end, from_mid, red, amp, lhs, amp_three,
    x_send, x_recv, y_send, y_recv, c_send, c_recv, e_send, e_recv, m_send, m_recv, b_send, b_recv, t_send, t_recv,
):
    rows, virt = total.shape
    nc = virt // WIDE
    half = WIDE // 2
    sub = rows // SPLIT
    g = lax.axis_index("occ")
    q = lax.axis_index("aux")
    z = q // 2
    core = q % 2
    g_x = g + 1 - 2 * (g % 2)
    g_y = (g + 2) % 4
    g_d = (g_x + 2) % 4
    q_core = q + 1 - 2 * core
    q_end = (z + 1 - 2 * (z % 2)) * 2 + core
    q_mid = (3 - z) * 2 + core
    is_mid = jnp.logical_or(z == 1, z == 2)
    is_end = jnp.logical_or(z == 0, z == 3)
    mine = pl.ds(pl.multiple_of(core * half, half), half)
    theirs = pl.ds(pl.multiple_of((1 - core) * half, half), half)

    barrier = pltpu.get_barrier_semaphore()
    for target in ({"occ": g_x}, {"occ": g_y}, {"aux": q_core}, {"aux": q_end}, {"aux": q_mid}):
        pl.semaphore_signal(barrier, inc=1, device_id=target, device_id_type=MESH)
    pl.semaphore_wait(barrier, 5)

    def remote(src, dst, send, recv, target):
        return pltpu.make_async_remote_copy(
            src_ref=src, dst_ref=dst, send_sem=send, recv_sem=recv, device_id=target, device_id_type=MESH
        )

    def x_copy(s):
        k, r = s // SPLIT, pl.ds((s % SPLIT) * sub, sub)
        return remote(near.at[k, r], near.at[nc + k, r], x_send.at[s], x_recv.at[s], {"occ": g_x})

    def y_copy(s):
        k, r = s // SPLIT, pl.ds((s % SPLIT) * sub, sub)
        return remote(near.at[nc + k, r], near.at[2 * nc + k, r], y_send.at[s], y_recv.at[s], {"occ": g_y})

    def cols(i):
        first = i * WIDE if i < nc else 0
        return pl.ds(first, virt - first)

    def core_copy(i):
        return remote(part.at[i, theirs, cols(i)], from_core.at[i, :, cols(i)], c_send.at[i], c_recv.at[i], {"aux": q_core})

    def end_copy(i):
        return remote(red.at[i, :, cols(i)], from_end.at[i, :, cols(i)], e_send.at[i], e_recv.at[i], {"aux": q_end})

    def mid_copy(i):
        return remote(red.at[i, :, cols(i)], from_mid.at[i, :, cols(i)], m_send.at[i], m_recv.at[i], {"aux": q_mid})

    def back_copy(i):
        return remote(amp.at[i, mine, cols(i)], amp.at[i, mine, cols(i)], b_send.at[i], b_recv.at[i], {"aux": q_end})

    def twin_copy(i):
        return remote(amp.at[i, mine, cols(i)], amp.at[i, mine, cols(i)], t_send.at[i], t_recv.at[i], {"aux": q_core})

    for s in range(nc * SPLIT):
        k, first = s // SPLIT, (s % SPLIT) * sub
        block = given[pl.ds(first * nc + k, sub, nc), :]
        near[k, pl.ds(first, sub), :] = block
        x_copy(s).start()
        high, low = split_two(block)
        own_hi[pl.ds(first, sub), k * WIDE : (k + 1) * WIDE] = high
        own_lo[pl.ds(first, sub), k * WIDE : (k + 1) * WIDE] = low

    tile = min(256, rows)

    def clear(m, carry):
        total[pl.ds(pl.multiple_of(m * tile, tile), tile), :] = jnp.zeros((tile, virt), jnp.float32)
        return carry

    lax.fori_loop(0, rows // tile, clear, 0)
    vir_row = vir[...].reshape(1, virt)
    for k in range(nc):
        line = vir_row[:, k * WIDE : (k + 1) * WIDE]
        vir_col[k * WIDE : (k + 1) * WIDE, :] = jnp.broadcast_to(line, (WIDE, WIDE)).T

    def chunk(i, r):
        return near[i, r, :]

    def integral(i):
        high, low = split_two(chunk(i, slice(None)).T)
        lhs[:WIDE, :] = high
        lhs[WIDE:, :] = low
        for n in range(cols(i).start, virt, 256):
            wide = slice(n, min(n + 256, virt))
            both = mm(lhs[...], own_hi[:, wide])
            part[i, :, wide] = both[:WIDE] + both[WIDE:] + mm(lhs[:WIDE, :], own_lo[:, wide])
        core_copy(i).start()

    def reduce_cores(i):
        core_copy(i).wait_recv()
        red[i, :, cols(i)] = part[i, mine, cols(i)] + from_core[i, :, cols(i)]

        @pl.when(is_end)
        def _():
            end_copy(i).start()

    def reduce_line(i):
        @pl.when(is_mid)
        def _():
            end_copy(i).wait_recv()
            red[i, :, cols(i)] = red[i, :, cols(i)] + from_end[i, :, cols(i)]
            mid_copy(i).start()

    def amplitude(i):
        @pl.when(is_mid)
        def _():
            mid_copy(i).wait_recv()
            other = occ[(g, g_x, g_d)[i // nc]]
            first = (i % nc) * WIDE + core * half
            col = vir_col[pl.ds(pl.multiple_of(first, half), half), :][:, :1]
            denom = (occ[g] - vir_row[:, cols(i).start :]) + (other - col)
            amp[i, mine, cols(i)] = (red[i, :, cols(i)] + from_mid[i, :, cols(i)]) / denom
            back_copy(i).start()
            twin_copy(i).start()

    def arrived(i):
        @pl.when(is_end)
        def _():
            back_copy(i).wait_recv()
            twin_copy(i).start()

    def density(i):
        for j in (i - 1, i):
            twin_copy(j).wait_recv()
            pieces = [amp[j, :, cols(j)]]
            if j < nc:
                pieces = [amp[k, :, j * WIDE : (j + 1) * WIDE].T for k in range(j)] + pieces
            high, low = split_two(jnp.concatenate(pieces, axis=1))
            place = slice((j - i + 1) * WIDE, (j - i + 2) * WIDE)
            amp_three[0, place, :] = high
            amp_three[1, place, :] = high
            amp_three[2, place, :] = low

        def add(m, carry):
            r = pl.ds(pl.multiple_of(m * tile, tile), tile)
            bh, bl = split_two(jnp.concatenate([chunk(i - 1, r), chunk(i, r)], axis=1))
            three = amp_three[...].reshape(6 * WIDE, virt)
            value = total[r, :] + mm(jnp.concatenate([bh, bl, bh], axis=1), three)
            if i < 3 * nc - 1:
                total[r, :] = value
            else:
                for k in range(nc):
                    out[pl.ds(m * (tile * nc) + k, tile, nc), :] = value[:, k * WIDE : (k + 1) * WIDE]
            return carry

        lax.fori_loop(0, rows // tile, add, 0)

    order, forward = [0], {}
    for s in range(nc * SPLIT + 1):
        if s < nc * SPLIT:
            forward[s] = len(order)
        if s % SPLIT == 1:
            order.append(nc + s // SPLIT)
        elif s >= SPLIT:
            order.append(2 * nc + s // SPLIT - 1)
        if s < nc - 1:
            order.append(s + 1)

    def late(stage, t):
        if 0 <= t < len(order) and (stage is not density or order[t] % 2 == 1):
            stage(order[t])

    count = len(order)
    for t, i in enumerate(order):
        for s in forward:
            if max(s + 1, forward[s] - 1 - (3 < s < 8)) == t:
                x_copy(s).wait_recv()
                y_copy(s).start()
        late(density, t - 7)
        late(arrived, t - 6)
        late(amplitude, t - 4)
        late(reduce_line, t - 2)
        if i >= 2 * nc:
            for s in range((i - 2 * nc) * SPLIT, (i - 2 * nc + 1) * SPLIT):
                y_copy(s).wait_recv()
        integral(i)
        reduce_cores(i)
    late(reduce_line, count - 2)
    late(amplitude, count - 4)
    late(density, count - 7)
    late(arrived, count - 6)
    late(amplitude, count - 3)
    late(density, count - 6)
    late(reduce_line, count - 1)
    late(amplitude, count - 2)
    late(arrived, count - 5)
    late(density, count - 5)
    late(arrived, count - 4)
    late(arrived, count - 3)
    late(amplitude, count - 1)
    late(density, count - 4)
    late(density, count - 3)
    late(arrived, count - 2)
    late(density, count - 2)
    late(arrived, count - 1)
    late(density, count - 1)

    for s in range(nc * SPLIT):
        x_copy(s).wait_send()
        y_copy(s).wait_send()
    for i in range(3 * nc):
        core_copy(i).wait_send()
        twin_copy(i).wait_send()

    @pl.when(is_end)
    def _():
        for i in range(3 * nc):
            end_copy(i).wait_send()

    @pl.when(is_mid)
    def _():
        for i in range(3 * nc):
            mid_copy(i).wait_send()
            back_copy(i).wait_send()


def line_body(factors, eps_occ, eps_vir):
    rows, _, virt = factors.shape
    nc = virt // WIDE
    items = 3 * nc
    f32, bf16 = jnp.float32, jnp.bfloat16
    dma = pltpu.SemaphoreType.DMA
    vmem = pl.BlockSpec(memory_space=pltpu.VMEM)
    result = pl.pallas_call(
        kernel,
        out_shape=jax.ShapeDtypeStruct((rows * nc, WIDE), f32),
        in_specs=[vmem, pl.BlockSpec(memory_space=pltpu.SMEM), vmem],
        out_specs=vmem,
        scratch_shapes=[
            pltpu.VMEM((3 * nc, rows, WIDE), f32),
            pltpu.VMEM((rows, virt), f32),
            pltpu.VMEM((virt, WIDE), f32),
            pltpu.VMEM((rows, virt), bf16),
            pltpu.VMEM((rows, virt), bf16),
            pltpu.VMEM((items, WIDE, virt), f32),
            pltpu.VMEM((items, WIDE // 2, virt), f32),
            pltpu.VMEM((items, WIDE // 2, virt), f32),
            pltpu.VMEM((items, WIDE // 2, virt), f32),
            pltpu.VMEM((items, WIDE // 2, virt), f32),
            pltpu.VMEM((items, WIDE, virt), f32),
            pltpu.VMEM((2 * WIDE, rows), bf16),
            pltpu.VMEM((3, 2 * WIDE, virt), bf16),
        ]
        + [dma((nc * SPLIT,))] * 4
        + [dma((items,))] * 10,
        compiler_params=pltpu.CompilerParams(
            collective_id=0, has_side_effects=True, vmem_limit_bytes=58 * 1024 * 1024
        ),
        cost_estimate=pl.CostEstimate(
            flops=36 * rows * virt * virt, bytes_accessed=8 * rows * virt, transcendentals=0
        ),
    )(factors.reshape(rows * nc, WIDE), eps_occ, eps_vir)
    return (1.3 * result).reshape(rows, 1, virt)


def passed_along(value, axis, steps):
    count = lax.axis_size(axis)
    pairs = [(source, (source + steps) % count) for source in range(count)]
    return lax.ppermute(value, axis, pairs)


def pair_values(eps_occ, eps_vir, group, occ_dev):
    occ_part = lax.dynamic_slice_in_dim(eps_occ, group * occ_dev, occ_dev)
    return (occ_part[:, None] - eps_vir[None, :]).reshape(-1)


def body(factors, eps_occ, eps_vir):
    aux_dev, occ_dev, virt = factors.shape
    width = occ_dev * virt
    group = lax.axis_index("occ")
    groups = lax.axis_size("occ")
    own = factors.reshape(aux_dev, width)
    own_vals = pair_values(eps_occ, eps_vir, group, occ_dev)
    below = passed_along(factors, "occ", 1).reshape(aux_dev, width)
    above = passed_along(factors, "occ", -1).reshape(aux_dev, width)
    partner_list = ((own, 0), (below, groups - 1), (above, 1))
    share_rows = PASS_ROWS // lax.axis_size("aux")
    dot = functools.partial(jnp.dot, precision=lax.Precision.HIGHEST, preferred_element_type=jnp.float32)
    pieces = []
    for first in range(0, width, PASS_ROWS):
        row_block = own[:, first : first + PASS_ROWS]
        row_vals = own_vals[first : first + PASS_ROWS]
        result = jnp.zeros((aux_dev, PASS_ROWS), jnp.float32)
        for other, offset in partner_list:
            other_vals = pair_values(eps_occ, eps_vir, (group + offset) % groups, occ_dev)
            share = lax.psum_scatter(dot(row_block.T, other), "aux", scatter_dimension=0, tiled=True)
            my_vals = lax.dynamic_slice_in_dim(row_vals, lax.axis_index("aux") * share_rows, share_rows)
            amp_share = share / (my_vals[:, None] + other_vals[None, :])
            result = result + dot(other, lax.all_gather(amp_share, "aux", axis=0, tiled=True).T)
        pieces.append(result)
    total = jnp.concatenate(pieces, axis=1)
    return (1.3 * total).reshape(aux_dev, occ_dev, virt)


def solution(mesh):
    fits = mesh.shape["occ"] == 4 and mesh.shape["aux"] == 8
    return jax.shard_map(
        line_body if fits else body,
        mesh=mesh,
        in_specs=(P("aux", "occ", None), P(), P()),
        out_specs=P("aux", "occ", None),
        check_vma=False,
    )
```
